256 devices in a mesh: fibre: 8 (over z), cols: 32 (over y, x, core).
Axes of the slice: x: 4, y: 4, z: 8, core: 2. Of those that a mesh axis runs over, the one named last changes fastest.
Arguments:
- tensor: float32 [512, 32, 8, 2048], P('fibre', 'cols'), may hold values from -6 to 6
- initial: float32 [512, 64], replicated, may hold values from -6 to 6
Outputs:
- core_slab: float32 [64, 32, 8, 2048], P(None, 'cols', 'fibre')
- basis: float32 [512, 64], replicated
The draws below stay inside these ranges and needn't reach their ends.
All inputs are finite; a program needn't handle non-finite values.
Results may differ from the reference program's by a relative error of at most 0.0002.
Values sent between devices are 32-bit elements; how exact they have to be, the bound alone decides.
A program may use at most 64 MiB of HBM per device.

```python
import jax
import jax.numpy as jnp
from jax import lax

M = 512
RANK = 64
COLS_DEV = 2048
ITERS = 2
N_FIBRE = 8
N_COLS = 32


def level_of(key, extent, split, least, top_value):
    level, own = 1.0, jax.random.fold_in(key, 6)
    for position, blocks in split:
        draws = jnp.exp(jax.random.uniform(jax.random.fold_in(own, position), (blocks,), jnp.float32, least / len(split), top_value / len(split)))
        level = level * jnp.repeat(draws, extent[position] // blocks).reshape([-1 if axis == position else 1 for axis in range(len(extent))])
    return level


def centred(rng, dims, deviation, most, pieces=(), held_as=jnp.bfloat16):
    drawn = jax.random.normal(rng, dims, jnp.float32) * deviation
    if len(pieces) > 0:
        drawn = level_of(rng, dims, pieces, -0.22, 0.18) * drawn
    return jnp.clip(drawn, min=-most, max=most).astype(held_as)


def setup_inputs(seed: int = 0) -> dict:
    seeds = jax.random.split(jax.random.key(seed), 3)
    tensor = centred(seeds[0], (M, N_COLS, N_FIBRE, COLS_DEV), 1.0, 6.0, ((0, 8), (1, 32)), jnp.float32)
    initial = centred(seeds[1], (M, RANK), 1.0, 6.0, (), jnp.float32)
    return dict(tensor=tensor, initial=initial)


def orthonormal(product):
    squares = jnp.dot(product.T, product, precision=lax.Precision.HIGHEST)
    lower = jnp.linalg.cholesky(squares)
    return lax.linalg.triangular_solve(lower, product, left_side=False, lower=True, transpose_a=True)

def reference(tensor, initial):
    modes = tensor.shape[0]
    matrix = tensor.reshape(modes, -1)
    gram = jnp.dot(matrix, matrix.T, precision=lax.Precision.HIGHEST)
    basis = initial
    for step in range(ITERS):
        basis = orthonormal(jnp.dot(gram, basis, precision=lax.Precision.HIGHEST))
    core_slab = jnp.dot(basis.T, matrix, precision=lax.Precision.HIGHEST)
    core_slab = core_slab.reshape(RANK, N_COLS, N_FIBRE, COLS_DEV)
    return (core_slab, basis)
```

```python
import jax
import jax.numpy as jnp
from jax import lax
from jax.experimental import pallas as pl
from jax.experimental.pallas import tpu as pltpu
from jax.sharding import PartitionSpec as P

MESH = pl.DeviceIdType.MESH
HIGHEST = lax.Precision.HIGHEST
F32 = jnp.float32

M = 512
RANK = 64
WIDTH = 2048
NZ = 8
ROWS = M // NZ
CHIPS = 16
CHUNKS = 8
CW = WIDTH // CHUNKS
HALF = M // 2
SLAB = HALF // CHIPS
LANES = 128
OFFSETS = (4, 3, 5, 2, 6, 1, 7)


def dot(a, b, contract):
    return lax.dot_general(
        a, b, (contract, ((), ())), precision=HIGHEST, preferred_element_type=F32
    )


def inverse_factor(squares):
    rows = lax.broadcasted_iota(jnp.int32, (RANK, LANES), 0)
    lanes = lax.broadcasted_iota(jnp.int32, (RANK, LANES), 1)
    start = jnp.where(lanes < RANK, squares, (lanes - RANK == rows).astype(F32))

    def panel(step, a):
        live = rows < RANK - 8 * step
        for t in range(8):
            scale = lax.rsqrt(a[t : t + 1, t : t + 1])
            row = a[t : t + 1, :] * scale
            column = a[:, t : t + 1] * scale
            update = jnp.where(live & (rows > t), a - column * row, a)
            a = jnp.where(rows == t, row, update)
        a = jnp.concatenate([a[8:], a[:8]], axis=0)
        return pltpu.roll(a, LANES - 8, 1)

    return lax.fori_loop(0, RANK // 8, panel, start)


def kernel(
    tensor,
    initial,
    slab_out,
    basis_out,
    stage,
    x,
    gram,
    core_in,
    half,
    plane_in,
    slab_g,
    z_y,
    z_g,
    own_y,
    y_all,
    own_w,
    w_all,
    load_sem,
    send_x,
    recv_x,
    send_p,
    recv_p,
    send_z,
    recv_z,
    send_c,
    recv_c,
):
    f, c = lax.axis_index("fibre"), lax.axis_index("cols")
    chip, core = c // 2, lax.rem(c, 2)
    chip_y, chip_x = chip // 4, lax.rem(chip, 4)
    other = 1 - core

    def z_at(offset):
        return lax.rem(f + offset, NZ)

    def chip_at(k):
        return lax.rem(chip_y + k // 4, 4) * 4 + lax.rem(chip_x + k % 4, 4)

    def send(src, dst, ssem, rsem, device):
        return pltpu.make_async_remote_copy(
            src_ref=src,
            dst_ref=dst,
            send_sem=ssem,
            recv_sem=rsem,
            device_id=device,
            device_id_type=MESH,
        )

    def load(j, g, to):
        columns = pl.ds(pl.multiple_of(j * CW, CW), CW)
        return pltpu.make_async_copy(
            tensor.at[:, 0, g, columns], to, load_sem.at[j, g]
        )

    def load_own(j):
        columns = pl.ds(pl.multiple_of(j * CW, CW), CW)
        return pltpu.make_async_copy(
            tensor.at[:, 0, f, columns], x.at[j, f], load_sem.at[j, NZ - 1]
        )

    @pl.loop(0, CHUNKS)
    def _(j):
        for i, offset in enumerate(OFFSETS):
            g = z_at(offset)
            pltpu.make_async_copy(
                tensor.at[:, 0, g, pl.ds(pl.multiple_of(j * CW, CW), CW)],
                stage.at[j, i],
                load_sem.at[j, i],
            ).start()
        load_own(j).start()

    barrier = pltpu.get_barrier_semaphore()
    for offset in OFFSETS:
        pl.semaphore_signal(
            barrier, inc=1, device_id=(z_at(offset), c), device_id_type=MESH
        )
    for k in range(1, CHIPS):
        pl.semaphore_signal(
            barrier, inc=1, device_id=(f, chip_at(k) * 2 + core), device_id_type=MESH
        )
    sibling = (f, chip * 2 + other)
    pl.semaphore_signal(barrier, inc=1, device_id=sibling, device_id_type=MESH)
    pl.semaphore_wait(barrier, NZ - 1 + CHIPS)

    def exchange(j, i):
        return send(
            stage.at[j, i],
            x.at[j, f],
            send_x.at[j, i],
            recv_x.at[j, i],
            (z_at(OFFSETS[i]), c),
        )

    @pl.loop(0, CHUNKS)
    def _(j):
        for i, offset in enumerate(OFFSETS):
            pltpu.make_async_copy(
                tensor.at[:, 0, z_at(offset), pl.ds(pl.multiple_of(j * CW, CW), CW)],
                stage.at[j, i],
                load_sem.at[j, i],
            ).wait()
            exchange(j, i).start()

    gram[...] = jnp.zeros_like(gram)

    @pl.loop(0, CHUNKS)
    def _(j):
        load_own(j).wait()
        for i in range(NZ - 1):
            exchange(j, i).wait_recv()
        block = x[j].reshape(M, CW)
        gram[...] += dot(block, block, ((1,), (1,)))

    mine = pl.ds(pl.multiple_of(core * HALF, HALF), HALF)
    theirs = pl.ds(pl.multiple_of(other * HALF, HALF), HALF)
    swap = send(gram.at[theirs], core_in, send_c.at[0], recv_c.at[0], sibling)
    swap.start()
    swap.wait_recv()
    half[...] = gram[mine] + core_in[...]

    def scatter(k):
        to = chip_at(k)
        return send(
            half.at[pl.ds(pl.multiple_of(to * SLAB, SLAB), SLAB)],
            plane_in.at[k],
            send_p.at[0, k],
            recv_p.at[0, k],
            (f, to * 2 + core),
        )

    for k in range(1, CHIPS):
        scatter(k).start()
    total = half[pl.ds(pl.multiple_of(chip * SLAB, SLAB), SLAB)]
    for k in range(1, CHIPS):
        scatter(k).wait_recv()
        total = total + plane_in[k]
    slab_g[...] = total

    start = initial[...]
    part = dot(total, start, ((1,), (1,)))
    own_y[0] = jnp.concatenate([part, jnp.zeros_like(part)], axis=1)

    def z_send_y(i):
        return send(
            own_y.at[0], z_y.at[i], send_z.at[0, i], recv_z.at[0, i], (z_at(OFFSETS[i]), c)
        )

    def z_send_g(i):
        return send(
            slab_g, z_g.at[i], send_z.at[1, i], recv_z.at[1, i], (z_at(OFFSETS[i]), c)
        )

    for i in range(NZ - 1):
        z_send_y(i).start()
    for i in range(NZ - 1):
        z_send_g(i).start()

    def z_sum(own, of):
        acc = None
        for z in range(NZ):
            value = own
            for i, offset in enumerate(OFFSETS):
                value = jnp.where(lax.rem(z + offset, NZ) == f, of[i], value)
            acc = value if acc is None else acc + value
        return acc

    for i in range(NZ - 1):
        z_send_y(i).wait_recv()
    own_y[1] = z_sum(own_y[0], z_y)

    def gather(own, whole, which):
        at = pl.ds(pl.multiple_of(chip * SLAB, SLAB), SLAB)
        whole[core, at] = own[...]

        def to_chip(k):
            return send(
                own,
                whole.at[core, at],
                send_p.at[1 + which, k],
                recv_p.at[1 + which, k],
                (f, chip_at(k) * 2 + core),
            )

        for k in range(1, CHIPS):
            to_chip(k).start()
        for k in range(1, CHIPS):
            to_chip(k).wait_recv()
        swap = send(
            whole.at[core], whole.at[core], send_c.at[1 + which], recv_c.at[1 + which], sibling
        )
        swap.start()
        sends.extend(to_chip(k) for k in range(1, CHIPS))
        sends.append(swap)
        return swap

    sends = [swap]
    gather(own_y.at[1], y_all, 0).wait_recv()
    y1 = y_all[...].reshape(M, LANES)

    for i in range(NZ - 1):
        z_send_g(i).wait_recv()
    own_g = z_sum(slab_g[...], z_g)
    own_w[...] = dot(own_g, y1, ((1,), (0,)))
    inverse1 = inverse_factor(dot(y1, y1, ((0,), (0,)))[:RANK])
    gather(own_w, w_all, 1).wait_recv()

    w = w_all[...].reshape(M, LANES)[:, :RANK]
    y2 = dot(w, inverse1[:, :RANK], ((1,), (1,)))
    squares = dot(y2, y2, ((0,), (0,)))
    inverse2 = inverse_factor(jnp.concatenate([squares, squares], axis=1))
    basis = dot(inverse2[:, :RANK], y2, ((1,), (1,)))
    basis_out[...] = basis

    for j in range(CHUNKS):
        slab_out[:, j * CW : (j + 1) * CW] = dot(
            basis, x[j].reshape(M, CW), ((1,), (0,))
        )

    @pl.loop(0, CHUNKS)
    def _(j):
        for i in range(NZ - 1):
            exchange(j, i).wait_send()

    for k in range(1, CHIPS):
        scatter(k).wait_send()
    for i in range(NZ - 1):
        z_send_y(i).wait_send()
        z_send_g(i).wait_send()
    for copy in sends:
        copy.wait_send()


def shards(tensor, initial):
    vmem = pl.BlockSpec(memory_space=pltpu.VMEM)
    slab, basis = pl.pallas_call(
        kernel,
        name="subspace",
        out_shape=(
            jax.ShapeDtypeStruct((RANK, WIDTH), F32),
            jax.ShapeDtypeStruct((RANK, M), F32),
        ),
        in_specs=[pl.BlockSpec(memory_space=pl.ANY), vmem],
        out_specs=(vmem, vmem),
        scratch_shapes=[
            pltpu.VMEM((CHUNKS, NZ - 1, ROWS, CW), F32),
            pltpu.VMEM((CHUNKS, NZ, ROWS, CW), F32),
            pltpu.VMEM((M, M), F32),
            pltpu.VMEM((HALF, M), F32),
            pltpu.VMEM((HALF, M), F32),
            pltpu.VMEM((CHIPS, SLAB, M), F32),
            pltpu.VMEM((SLAB, M), F32),
            pltpu.VMEM((NZ - 1, SLAB, LANES), F32),
            pltpu.VMEM((NZ - 1, SLAB, M), F32),
            pltpu.VMEM((2, SLAB, LANES), F32),
            pltpu.VMEM((2, HALF, LANES), F32),
            pltpu.VMEM((SLAB, LANES), F32),
            pltpu.VMEM((2, HALF, LANES), F32),
            pltpu.SemaphoreType.DMA((CHUNKS, NZ)),
            pltpu.SemaphoreType.DMA((CHUNKS, NZ - 1)),
            pltpu.SemaphoreType.DMA((CHUNKS, NZ - 1)),
            pltpu.SemaphoreType.DMA((3, CHIPS)),
            pltpu.SemaphoreType.DMA((3, CHIPS)),
            pltpu.SemaphoreType.DMA((2, NZ - 1)),
            pltpu.SemaphoreType.DMA((2, NZ - 1)),
            pltpu.SemaphoreType.DMA((3,)),
            pltpu.SemaphoreType.DMA((3,)),
        ],
        compiler_params=pltpu.CompilerParams(
            collective_id=0, has_side_effects=True, vmem_limit_bytes=56 * 1024 * 1024
        ),
    )(tensor, initial.T)
    return slab.reshape(RANK, 1, 1, WIDTH), basis.T


def solution(mesh):
    return jax.shard_map(
        shards,
        mesh=mesh,
        in_specs=(P("fibre", "cols", None, None), P()),
        out_specs=(P(None, "cols", "fibre", None), P()),
        check_vma=False,
    )
```

```python
import jax
import jax.numpy as jnp
from jax import lax
from jax.experimental import pallas as pl
from jax.experimental.pallas import tpu as pltpu
from jax.sharding import PartitionSpec as P

MESH = pl.DeviceIdType.MESH
HIGHEST = lax.Precision.HIGHEST
F32 = jnp.float32

M = 512
RANK = 64
WIDTH = 2048
NZ = 8
ROWS = M // NZ
CHIPS = 16
CHUNKS = 8
CW = WIDTH // CHUNKS
HALF = M // 2
SLAB = HALF // CHIPS
LANES = 128
OFFSETS = (4, 3, 5, 2, 6, 1, 7)


def dot(a, b, contract):
    return lax.dot_general(
        a, b, (contract, ((), ())), precision=HIGHEST, preferred_element_type=F32
    )


def augmented(squares):
    rows = lax.broadcasted_iota(jnp.int32, (RANK, LANES), 0)
    lanes = lax.broadcasted_iota(jnp.int32, (RANK, LANES), 1)
    return jnp.where(lanes < RANK, squares, (lanes - RANK == rows).astype(F32))


def eliminate(start, first, last):
    rows = lax.broadcasted_iota(jnp.int32, (RANK, LANES), 0)

    def panel(step, a):
        live = rows < RANK - 8 * step
        for t in range(8):
            scale = lax.rsqrt(a[t : t + 1, t : t + 1])
            row = a[t : t + 1, :] * scale
            column = a[:, t : t + 1] * scale
            update = jnp.where(live & (rows > t), a - column * row, a)
            a = jnp.where(rows == t, row, update)
        a = jnp.concatenate([a[8:], a[:8]], axis=0)
        return pltpu.roll(a, LANES - 8, 1)

    return lax.fori_loop(first, last, panel, start)


def kernel(
    tensor,
    initial,
    slab_out,
    basis_out,
    stage,
    x,
    gram,
    core_in,
    half,
    plane_in,
    slab_g,
    z_y,
    z_g,
    own_y,
    y_all,
    own_w,
    w_all,
    load_sem,
    send_x,
    recv_x,
    send_p,
    recv_p,
    send_z,
    recv_z,
    send_c,
    recv_c,
):
    f, c = lax.axis_index("fibre"), lax.axis_index("cols")
    chip, core = c // 2, lax.rem(c, 2)
    chip_y, chip_x = chip // 4, lax.rem(chip, 4)
    other = 1 - core

    def z_at(offset):
        return lax.rem(f + offset, NZ)

    def chip_at(k):
        return lax.rem(chip_y + k // 4, 4) * 4 + lax.rem(chip_x + k % 4, 4)

    def send(src, dst, ssem, rsem, device):
        return pltpu.make_async_remote_copy(
            src_ref=src,
            dst_ref=dst,
            send_sem=ssem,
            recv_sem=rsem,
            device_id=device,
            device_id_type=MESH,
        )

    def load(j, g, to):
        columns = pl.ds(pl.multiple_of(j * CW, CW), CW)
        return pltpu.make_async_copy(
            tensor.at[:, 0, g, columns], to, load_sem.at[j, g]
        )

    def load_own(j):
        columns = pl.ds(pl.multiple_of(j * CW, CW), CW)
        return pltpu.make_async_copy(
            tensor.at[:, 0, f, columns], x.at[j, f], load_sem.at[j, NZ - 1]
        )

    @pl.loop(0, CHUNKS)
    def _(j):
        for i, offset in enumerate(OFFSETS):
            g = z_at(offset)
            pltpu.make_async_copy(
                tensor.at[:, 0, g, pl.ds(pl.multiple_of(j * CW, CW), CW)],
                stage.at[j, i],
                load_sem.at[j, i],
            ).start()
        load_own(j).start()

    barrier = pltpu.get_barrier_semaphore()
    for offset in OFFSETS:
        pl.semaphore_signal(
            barrier, inc=1, device_id=(z_at(offset), c), device_id_type=MESH
        )
    for k in range(1, CHIPS):
        pl.semaphore_signal(
            barrier, inc=1, device_id=(f, chip_at(k) * 2 + core), device_id_type=MESH
        )
    sibling = (f, chip * 2 + other)
    pl.semaphore_signal(barrier, inc=1, device_id=sibling, device_id_type=MESH)
    pl.semaphore_wait(barrier, NZ - 1 + CHIPS)

    def exchange(j, i):
        return send(
            stage.at[j, i],
            x.at[j, f],
            send_x.at[j, i],
            recv_x.at[j, i],
            (z_at(OFFSETS[i]), c),
        )

    @pl.loop(0, CHUNKS)
    def _(j):
        for i, offset in enumerate(OFFSETS):
            pltpu.make_async_copy(
                tensor.at[:, 0, z_at(offset), pl.ds(pl.multiple_of(j * CW, CW), CW)],
                stage.at[j, i],
                load_sem.at[j, i],
            ).wait()
            exchange(j, i).start()

    gram[...] = jnp.zeros_like(gram)

    @pl.loop(0, CHUNKS)
    def _(j):
        load_own(j).wait()
        for i in range(NZ - 1):
            exchange(j, i).wait_recv()
        block = x[j].reshape(M, CW)
        gram[...] += dot(block, block, ((1,), (1,)))

    mine = pl.ds(pl.multiple_of(core * HALF, HALF), HALF)
    theirs = pl.ds(pl.multiple_of(other * HALF, HALF), HALF)
    swap = send(gram.at[theirs], core_in, send_c.at[0], recv_c.at[0], sibling)
    swap.start()
    swap.wait_recv()
    half[...] = gram[mine] + core_in[...]

    def scatter(k):
        to = chip_at(k)
        return send(
            half.at[pl.ds(pl.multiple_of(to * SLAB, SLAB), SLAB)],
            plane_in.at[k],
            send_p.at[0, k],
            recv_p.at[0, k],
            (f, to * 2 + core),
        )

    for k in range(1, CHIPS):
        scatter(k).start()
    total = half[pl.ds(pl.multiple_of(chip * SLAB, SLAB), SLAB)]
    for k in range(1, CHIPS):
        scatter(k).wait_recv()
        total = total + plane_in[k]
    slab_g[...] = total

    start = initial[...]
    part = dot(total, start, ((1,), (1,)))
    own_y[0] = jnp.concatenate([part, jnp.zeros_like(part)], axis=1)

    def z_send_y(i):
        return send(
            own_y.at[0], z_y.at[i], send_z.at[0, i], recv_z.at[0, i], (z_at(OFFSETS[i]), c)
        )

    def z_send_g(i):
        return send(
            slab_g, z_g.at[i], send_z.at[1, i], recv_z.at[1, i], (z_at(OFFSETS[i]), c)
        )

    for i in range(NZ - 1):
        z_send_y(i).start()
    for i in range(NZ - 1):
        z_send_g(i).start()

    def z_sum(own, of):
        acc = None
        for z in range(NZ):
            value = own
            for i, offset in enumerate(OFFSETS):
                value = jnp.where(lax.rem(z + offset, NZ) == f, of[i], value)
            acc = value if acc is None else acc + value
        return acc

    for i in range(NZ - 1):
        z_send_y(i).wait_recv()
    own_y[1] = z_sum(own_y[0], z_y)

    at = pl.ds(pl.multiple_of(chip * SLAB, SLAB), SLAB)

    def to_chip(own, whole, which, k):
        return send(
            own,
            whole.at[core, at],
            send_p.at[which, k],
            recv_p.at[which, k],
            (f, chip_at(k) * 2 + core),
        )

    def to_core(whole, which):
        return send(
            whole.at[core], whole.at[core], send_c.at[which], recv_c.at[which], sibling
        )

    def gather_start(own, whole, which):
        for k in range(1, CHIPS):
            to_chip(own, whole, which, k).start()
        whole[core, at] = own[...]

    def gather_swap(own, whole, which):
        for k in range(1, CHIPS):
            to_chip(own, whole, which, k).wait_recv()
        to_core(whole, which).start()

    gather_start(own_y.at[1], y_all, 1)
    gather_swap(own_y.at[1], y_all, 1)
    for i in range(NZ - 1):
        z_send_g(i).wait_recv()
    own_g = z_sum(slab_g[...], z_g)
    to_core(y_all, 1).wait_recv()
    y1 = y_all[...].reshape(M, LANES)
    own_w[...] = dot(own_g, y1, ((1,), (0,)))
    gather_start(own_w, w_all, 2)
    partial = eliminate(augmented(dot(y1, y1, ((0,), (0,)))[:RANK]), 0, 6)
    gather_swap(own_w, w_all, 2)
    inverse1 = eliminate(partial, 6, 8)
    to_core(w_all, 2).wait_recv()

    w = w_all[...].reshape(M, LANES)[:, :RANK]
    y2 = dot(w, inverse1[:, :RANK], ((1,), (1,)))
    squares = dot(y2, y2, ((0,), (0,)))
    inverse2 = eliminate(augmented(jnp.concatenate([squares, squares], axis=1)), 0, 8)
    basis = dot(inverse2[:, :RANK], y2, ((1,), (1,)))
    basis_out[...] = basis

    for j in range(CHUNKS):
        slab_out[:, j * CW : (j + 1) * CW] = dot(
            basis, x[j].reshape(M, CW), ((1,), (0,))
        )

    @pl.loop(0, CHUNKS)
    def _(j):
        for i in range(NZ - 1):
            exchange(j, i).wait_send()

    for k in range(1, CHIPS):
        scatter(k).wait_send()
    for i in range(NZ - 1):
        z_send_y(i).wait_send()
        z_send_g(i).wait_send()
    for k in range(1, CHIPS):
        to_chip(own_y.at[1], y_all, 1, k).wait_send()
        to_chip(own_w, w_all, 2, k).wait_send()
    swap.wait_send()
    to_core(y_all, 1).wait_send()
    to_core(w_all, 2).wait_send()


def shards(tensor, initial):
    vmem = pl.BlockSpec(memory_space=pltpu.VMEM)
    slab, basis = pl.pallas_call(
        kernel,
        name="subspace",
        out_shape=(
            jax.ShapeDtypeStruct((RANK, WIDTH), F32),
            jax.ShapeDtypeStruct((RANK, M), F32),
        ),
        in_specs=[pl.BlockSpec(memory_space=pl.ANY), vmem],
        out_specs=(vmem, vmem),
        scratch_shapes=[
            pltpu.VMEM((CHUNKS, NZ - 1, ROWS, CW), F32),
            pltpu.VMEM((CHUNKS, NZ, ROWS, CW), F32),
            pltpu.VMEM((M, M), F32),
            pltpu.VMEM((HALF, M), F32),
            pltpu.VMEM((HALF, M), F32),
            pltpu.VMEM((CHIPS, SLAB, M), F32),
            pltpu.VMEM((SLAB, M), F32),
            pltpu.VMEM((NZ - 1, SLAB, LANES), F32),
            pltpu.VMEM((NZ - 1, SLAB, M), F32),
            pltpu.VMEM((2, SLAB, LANES), F32),
            pltpu.VMEM((2, HALF, LANES), F32),
            pltpu.VMEM((SLAB, LANES), F32),
            pltpu.VMEM((2, HALF, LANES), F32),
            pltpu.SemaphoreType.DMA((CHUNKS, NZ)),
            pltpu.SemaphoreType.DMA((CHUNKS, NZ - 1)),
            pltpu.SemaphoreType.DMA((CHUNKS, NZ - 1)),
            pltpu.SemaphoreType.DMA((3, CHIPS)),
            pltpu.SemaphoreType.DMA((3, CHIPS)),
            pltpu.SemaphoreType.DMA((2, NZ - 1)),
            pltpu.SemaphoreType.DMA((2, NZ - 1)),
            pltpu.SemaphoreType.DMA((3,)),
            pltpu.SemaphoreType.DMA((3,)),
        ],
        compiler_params=pltpu.CompilerParams(
            collective_id=0, has_side_effects=True, vmem_limit_bytes=51 * 1024 * 1024
        ),
    )(tensor, initial.T)
    return slab.reshape(RANK, 1, 1, WIDTH), basis.T


def solution(mesh):
    return jax.shard_map(
        shards,
        mesh=mesh,
        in_specs=(P("fibre", "cols", None, None), P()),
        out_specs=(P(None, "cols", "fibre", None), P()),
        check_vma=False,
    )
```

```python
import jax
import jax.numpy as jnp
from jax import lax
from jax.experimental import pallas as pl
from jax.experimental.pallas import tpu as pltpu
from jax.sharding import PartitionSpec as P

MESH = pl.DeviceIdType.MESH
HIGHEST = lax.Precision.HIGHEST
F32 = jnp.float32

M = 512
RANK = 64
WIDTH = 2048
NZ = 8
ROWS = M // NZ
CHIPS = 16
CHUNKS = 16
CW = WIDTH // CHUNKS
HALF = M // 2
SLAB = HALF // CHIPS
LANES = 128
OFFSETS = (4, 3, 5, 2, 6, 1, 7)


def dot(a, b, contract):
    return lax.dot_general(
        a, b, (contract, ((), ())), precision=HIGHEST, preferred_element_type=F32
    )


def augmented(squares):
    rows = lax.broadcasted_iota(jnp.int32, (RANK, LANES), 0)
    lanes = lax.broadcasted_iota(jnp.int32, (RANK, LANES), 1)
    return jnp.where(lanes < RANK, squares, (lanes - RANK == rows).astype(F32))


def inverse_factor(squares):
    rows = lax.broadcasted_iota(jnp.int32, (RANK, LANES), 0)
    top = lax.broadcasted_iota(jnp.int32, (8, LANES), 0)

    def panel(step, a):
        live = rows < RANK - 8 * step
        columns = [
            jnp.where(live, jnp.broadcast_to(a[:, t : t + 1], (RANK, LANES)), 0.0)
            for t in range(8)
        ]
        for t in range(8):
            pivot = columns[t][t : t + 1]
            inverse = 1.0 / pivot
            column = jnp.where(rows > t, columns[t], 0.0)
            row = a[t : t + 1]
            for q in range(t + 1, 8):
                columns[q] = columns[q] - column * (columns[q][t : t + 1] * inverse)
            a = a - column * (row * inverse)
            head = jnp.where(top == t, row * lax.rsqrt(pivot), a[:8])
            a = jnp.concatenate([head, a[8:]], axis=0)
        a = jnp.concatenate([a[8:], a[:8]], axis=0)
        return pltpu.roll(a, LANES - 8, 1)

    return lax.fori_loop(0, RANK // 8, panel, augmented(squares))[:, :RANK]


def pack(y):
    y = y.reshape(y.shape[0] // 16, 2, 8, RANK)
    return jnp.concatenate([y[:, 0], y[:, 1]], axis=2)


def unpack(y):
    n = y.shape[0]
    y = jnp.stack([y[:, :, :RANK], y[:, :, RANK:]], axis=1)
    return y.reshape(16 * n, RANK)


def kernel(
    tensor,
    initial,
    slab_out,
    basis_out,
    x,
    gram,
    core_g,
    half_g,
    plane_g,
    slab_g,
    z_g,
    part_y,
    core_y,
    half_y,
    plane_y,
    z_y,
    own_y,
    y_all,
    w_all,
    load_sem,
    send_x,
    recv_x,
    send_p,
    recv_p,
    send_z,
    recv_z,
    send_c,
    recv_c,
):
    f, c = lax.axis_index("fibre"), lax.axis_index("cols")
    chip, core = c // 2, lax.rem(c, 2)
    chip_y, chip_x = chip // 4, lax.rem(chip, 4)
    other = 1 - core
    sibling = (f, chip * 2 + other)

    def z_at(offset):
        return lax.rem(f + offset, NZ)

    def chip_at(k):
        return lax.rem(chip_y + k // 4, 4) * 4 + lax.rem(chip_x + k % 4, 4)

    def send(src, dst, ssem, rsem, device):
        return pltpu.make_async_remote_copy(
            src_ref=src,
            dst_ref=dst,
            send_sem=ssem,
            recv_sem=rsem,
            device_id=device,
            device_id_type=MESH,
        )

    def piece(j, z):
        return tensor.at[:, 0, z, pl.ds(pl.multiple_of(j * CW, CW), CW)]

    def load_own(j):
        return pltpu.make_async_copy(piece(j, f), x.at[j, f], load_sem.at[j])

    def exchange(j, i):
        to = z_at(OFFSETS[i])
        return send(
            piece(j, to), x.at[j, f], send_x.at[j, i], recv_x.at[j, i], (to, c)
        )

    def to_core(src, dst, which):
        return send(src, dst, send_c.at[which], recv_c.at[which], sibling)

    def to_chip(src, dst, which, k):
        return send(
            src,
            dst,
            send_p.at[which, k],
            recv_p.at[which, k],
            (f, chip_at(k) * 2 + core),
        )

    def to_z(src, dst, which, i):
        return send(
            src, dst, send_z.at[which, i], recv_z.at[which, i], (z_at(OFFSETS[i]), c)
        )

    def each(count, start, make, act):
        for k in range(start, count):
            act(make(k))

    def started(copy):
        copy.start()

    def arrived(copy):
        copy.wait_recv()

    def left(copy):
        copy.wait_send()

    barrier = pltpu.get_barrier_semaphore()
    for offset in OFFSETS:
        pl.semaphore_signal(
            barrier, inc=1, device_id=(z_at(offset), c), device_id_type=MESH
        )
    for k in range(1, CHIPS):
        pl.semaphore_signal(
            barrier, inc=1, device_id=(f, chip_at(k) * 2 + core), device_id_type=MESH
        )
    pl.semaphore_signal(barrier, inc=1, device_id=sibling, device_id_type=MESH)

    @pl.loop(0, CHUNKS)
    def _(j):
        load_own(j).start()

    gram[...] = jnp.zeros_like(gram)
    pl.semaphore_wait(barrier, NZ - 1 + CHIPS)

    @pl.loop(0, CHUNKS)
    def _(j):
        for i in range(NZ - 1):
            exchange(j, i).start()

    start = initial[...]

    def chunk_arrived(j):
        load_own(j).wait()
        for i in range(NZ - 1):
            exchange(j, i).wait_recv()

    @pl.loop(0, CHUNKS - 1)
    def _(j):
        chunk_arrived(j)
        block = x[j].reshape(M, CW)
        gram[...] += dot(block, block, ((1,), (1,)))

    early = dot(gram[...], start, ((1,), (1,)))
    chunk_arrived(CHUNKS - 1)
    block = x[CHUNKS - 1].reshape(M, CW)
    late = dot(block, dot(start, block, ((1,), (0,))), ((1,), (1,)))
    part_y[...] = pack(early + late).reshape(2, CHIPS, 8, LANES)

    swap_y = to_core(part_y.at[other], core_y, 0)
    swap_y.start()
    gram[...] += dot(block, block, ((1,), (1,)))
    mine = pl.ds(pl.multiple_of(core * HALF, HALF), HALF)
    theirs = pl.ds(pl.multiple_of(other * HALF, HALF), HALF)
    swap_g = to_core(gram.at[theirs], core_g, 1)
    swap_g.start()

    swap_y.wait_recv()
    half_y[...] = part_y[core] + core_y[...]

    def scatter_y(k):
        return to_chip(half_y.at[chip_at(k)], plane_y.at[k], 0, k)

    each(CHIPS, 1, scatter_y, started)

    swap_g.wait_recv()
    half_g[...] = gram[mine] + core_g[...]

    def scatter_g(k):
        rows = pl.ds(pl.multiple_of(chip_at(k) * SLAB, SLAB), SLAB)
        return to_chip(half_g.at[rows], plane_g.at[k], 1, k)

    each(CHIPS, 1, scatter_g, started)

    each(CHIPS, 1, scatter_y, arrived)
    total = half_y[chip]
    for k in range(1, CHIPS):
        total = total + plane_y[k]
    own_y[0] = total

    def z_send_y(i):
        return to_z(own_y.at[0], z_y.at[i], 0, i)

    each(NZ - 1, 0, z_send_y, started)

    def z_sum(own, of):
        acc = None
        for z in range(NZ):
            value = own
            for i, offset in enumerate(OFFSETS):
                value = jnp.where(lax.rem(z + offset, NZ) == f, of[i], value)
            acc = value if acc is None else acc + value
        return acc

    each(NZ - 1, 0, z_send_y, arrived)
    own_y[1] = z_sum(own_y[0], z_y)

    def gather_y(k):
        return to_chip(own_y.at[1], y_all.at[core, chip], 2, k)

    def gather_w(k):
        return to_chip(own_y.at[2], w_all.at[core, chip], 3, k)

    each(CHIPS, 1, gather_y, started)
    y_all[core, chip] = own_y[1]

    each(CHIPS, 1, scatter_g, arrived)
    total = half_g[pl.ds(pl.multiple_of(chip * SLAB, SLAB), SLAB)]
    for k in range(1, CHIPS):
        total = total + plane_g[k]
    slab_g[...] = total

    def z_send_g(i):
        return to_z(slab_g, z_g.at[i], 1, i)

    each(NZ - 1, 0, z_send_g, started)

    each(CHIPS, 1, gather_y, arrived)
    join_y = to_core(y_all.at[core], y_all.at[core], 2)
    join_y.start()
    join_y.wait_recv()
    y1 = unpack(y_all[...].reshape(2 * CHIPS, 8, LANES))
    squares = dot(y1, y1, ((0,), (0,)))
    inverse1 = inverse_factor(jnp.concatenate([squares, squares], axis=1))

    each(NZ - 1, 0, z_send_g, arrived)
    own_g = z_sum(slab_g[...], z_g)
    own_y[2] = pack(dot(own_g, y1, ((1,), (0,))))[0]
    each(CHIPS, 1, gather_w, started)
    w_all[core, chip] = own_y[2]
    each(CHIPS, 1, gather_w, arrived)
    join_w = to_core(w_all.at[core], w_all.at[core], 3)
    join_w.start()
    join_w.wait_recv()

    w = unpack(w_all[...].reshape(2 * CHIPS, 8, LANES))
    y2 = dot(inverse1, w, ((1,), (1,)))
    squares = dot(y2, y2, ((1,), (1,)))
    inverse2 = inverse_factor(jnp.concatenate([squares, squares], axis=1))
    basis = dot(inverse2, y2, ((1,), (0,)))
    basis_out[...] = basis

    for j in range(0, CHUNKS, 2):
        pair = jnp.concatenate([x[j].reshape(M, CW), x[j + 1].reshape(M, CW)], axis=1)
        slab_out[:, j * CW : (j + 2) * CW] = dot(basis, pair, ((1,), (0,)))

    @pl.loop(0, CHUNKS)
    def _(j):
        for i in range(NZ - 1):
            exchange(j, i).wait_send()

    for make in (scatter_y, scatter_g, gather_y, gather_w):
        each(CHIPS, 1, make, left)
    for make in (z_send_y, z_send_g):
        each(NZ - 1, 0, make, left)
    for copy in (swap_y, swap_g, join_y, join_w):
        copy.wait_send()


def shards(tensor, initial):
    vmem = pl.BlockSpec(memory_space=pltpu.VMEM)
    slab, basis = pl.pallas_call(
        kernel,
        name="subspace",
        out_shape=(
            jax.ShapeDtypeStruct((RANK, WIDTH), F32),
            jax.ShapeDtypeStruct((RANK, M), F32),
        ),
        in_specs=[pl.BlockSpec(memory_space=pl.ANY), vmem],
        out_specs=(vmem, vmem),
        scratch_shapes=[
            pltpu.VMEM((CHUNKS, NZ, ROWS, CW), F32),
            pltpu.VMEM((M, M), F32),
            pltpu.VMEM((HALF, M), F32),
            pltpu.VMEM((HALF, M), F32),
            pltpu.VMEM((CHIPS, SLAB, M), F32),
            pltpu.VMEM((SLAB, M), F32),
            pltpu.VMEM((NZ - 1, SLAB, M), F32),
            pltpu.VMEM((2, CHIPS, 8, LANES), F32),
            pltpu.VMEM((CHIPS, 8, LANES), F32),
            pltpu.VMEM((CHIPS, 8, LANES), F32),
            pltpu.VMEM((CHIPS, 8, LANES), F32),
            pltpu.VMEM((NZ - 1, 8, LANES), F32),
            pltpu.VMEM((3, 8, LANES), F32),
            pltpu.VMEM((2, CHIPS, 8, LANES), F32),
            pltpu.VMEM((2, CHIPS, 8, LANES), F32),
            pltpu.SemaphoreType.DMA((CHUNKS,)),
            pltpu.SemaphoreType.DMA((CHUNKS, NZ - 1)),
            pltpu.SemaphoreType.DMA((CHUNKS, NZ - 1)),
            pltpu.SemaphoreType.DMA((4, CHIPS)),
            pltpu.SemaphoreType.DMA((4, CHIPS)),
            pltpu.SemaphoreType.DMA((2, NZ - 1)),
            pltpu.SemaphoreType.DMA((2, NZ - 1)),
            pltpu.SemaphoreType.DMA((4,)),
            pltpu.SemaphoreType.DMA((4,)),
        ],
        compiler_params=pltpu.CompilerParams(
            collective_id=0, has_side_effects=True, vmem_limit_bytes=51 * 1024 * 1024
        ),
    )(tensor, initial.T)
    return slab.reshape(RANK, 1, 1, WIDTH), basis.T


def solution(mesh):
    return jax.shard_map(
        shards,
        mesh=mesh,
        in_specs=(P("fibre", "cols", None, None), P()),
        out_specs=(P(None, "cols", "fibre", None), P()),
        check_vma=False,
    )
```

```python
import jax
import jax.numpy as jnp
from jax import lax
from jax.experimental import pallas as pl
from jax.experimental.pallas import tpu as pltpu
from jax.sharding import PartitionSpec as P

MESH = pl.DeviceIdType.MESH
HIGHEST = lax.Precision.HIGHEST
F32 = jnp.float32

M = 512
RANK = 64
WIDTH = 2048
NZ = 8
ROWS = M // NZ
CHIPS = 16
CHUNKS = 16
CW = WIDTH // CHUNKS
HALF = M // 2
SLAB = HALF // CHIPS
LANES = 128
OFFSETS = (4, 3, 5, 2, 6, 1, 7)


def hops(k):
    return min(k // 4, 4 - k // 4) + min(k % 4, 4 - k % 4)


NEXT = tuple(sorted(range(1, CHIPS), key=hops, reverse=True))
PEERS = tuple((k, o) for k in NEXT for o in (0, 1)) + ((0, 1),)


def dot(a, b, contract):
    return lax.dot_general(
        a, b, (contract, ((), ())), precision=HIGHEST, preferred_element_type=F32
    )


def augmented(squares):
    rows = lax.broadcasted_iota(jnp.int32, (RANK, LANES), 0)
    lanes = lax.broadcasted_iota(jnp.int32, (RANK, LANES), 1)
    return jnp.where(lanes < RANK, squares, (lanes - RANK == rows).astype(F32))


def inverse_factor(squares):
    rows = lax.broadcasted_iota(jnp.int32, (RANK, LANES), 0)
    top = lax.broadcasted_iota(jnp.int32, (8, LANES), 0)

    def panel(step, a):
        live = rows < RANK - 8 * step
        columns = [
            jnp.where(live, jnp.broadcast_to(a[:, t : t + 1], (RANK, LANES)), 0.0)
            for t in range(8)
        ]
        for t in range(8):
            pivot = columns[t][t : t + 1]
            inverse = 1.0 / pivot
            column = jnp.where(rows > t, columns[t], 0.0)
            row = a[t : t + 1]
            for q in range(t + 1, 8):
                columns[q] = columns[q] - column * (columns[q][t : t + 1] * inverse)
            a = a - column * (row * inverse)
            head = jnp.where(top == t, row * lax.rsqrt(pivot), a[:8])
            a = jnp.concatenate([head, a[8:]], axis=0)
        a = jnp.concatenate([a[8:], a[:8]], axis=0)
        return pltpu.roll(a, LANES - 8, 1)

    return lax.fori_loop(0, RANK // 8, panel, augmented(squares))[:, :RANK]


def pack(y):
    y = y.reshape(y.shape[0] // 16, 2, 8, RANK)
    return jnp.concatenate([y[:, 0], y[:, 1]], axis=2)


def unpack(y):
    n = y.shape[0]
    y = jnp.stack([y[:, :, :RANK], y[:, :, RANK:]], axis=1)
    return y.reshape(16 * n, RANK)


def kernel(
    tensor,
    initial,
    slab_out,
    basis_out,
    x,
    gram,
    core_g,
    half_g,
    plane_g,
    slab_g,
    z_g,
    part_y,
    plane_y,
    z_y,
    own_y,
    y_all,
    w_all,
    load_sem,
    send_x,
    recv_x,
    send_p,
    recv_p,
    send_d,
    recv_d,
    send_z,
    recv_z,
    send_c,
    recv_c,
):
    f, c = lax.axis_index("fibre"), lax.axis_index("cols")
    chip, core = c // 2, lax.rem(c, 2)
    chip_y, chip_x = chip // 4, lax.rem(chip, 4)
    other = 1 - core
    sibling = (f, chip * 2 + other)

    def z_at(offset):
        return lax.rem(f + offset, NZ)

    def chip_at(k):
        return lax.rem(chip_y + k // 4, 4) * 4 + lax.rem(chip_x + k % 4, 4)

    def send(src, dst, ssem, rsem, device):
        return pltpu.make_async_remote_copy(
            src_ref=src,
            dst_ref=dst,
            send_sem=ssem,
            recv_sem=rsem,
            device_id=device,
            device_id_type=MESH,
        )

    def piece(j, z):
        return tensor.at[:, 0, z, pl.ds(pl.multiple_of(j * CW, CW), CW)]

    def load_own(j):
        return pltpu.make_async_copy(piece(j, f), x.at[j, f], load_sem.at[j])

    def exchange(j, i):
        to = z_at(OFFSETS[i])
        return send(
            piece(j, to), x.at[j, f], send_x.at[j, i], recv_x.at[j, i], (to, c)
        )

    def to_chip(src, dst, k):
        return send(
            src, dst, send_p.at[k], recv_p.at[k], (f, chip_at(k) * 2 + core)
        )

    def peer(n):
        k, o = PEERS[n]
        return chip_at(k), other if o else core

    def to_peer(src, dst, which, n):
        to, at = peer(n)
        return send(
            src, dst, send_d.at[which, n], recv_d.at[which, n], (f, to * 2 + at)
        )

    def to_z(src, dst, which, i):
        return send(
            src, dst, send_z.at[which, i], recv_z.at[which, i], (z_at(OFFSETS[i]), c)
        )

    def each(order, make, act):
        for k in order:
            act(make(k))

    def started(copy):
        copy.start()

    def arrived(copy):
        copy.wait_recv()

    def left(copy):
        copy.wait_send()

    barrier = pltpu.get_barrier_semaphore()
    for offset in OFFSETS:
        pl.semaphore_signal(
            barrier, inc=1, device_id=(z_at(offset), c), device_id_type=MESH
        )
    for n in range(len(PEERS)):
        to, at = peer(n)
        pl.semaphore_signal(
            barrier, inc=1, device_id=(f, to * 2 + at), device_id_type=MESH
        )

    @pl.loop(0, CHUNKS)
    def _(j):
        load_own(j).start()

    gram[...] = jnp.zeros_like(gram)
    pl.semaphore_wait(barrier, NZ - 1 + len(PEERS))

    @pl.loop(0, CHUNKS)
    def _(j):
        for i in range(NZ - 1):
            exchange(j, i).start()

    @pl.loop(0, CHUNKS)
    def _(j):
        load_own(j).wait()
        for i in range(NZ - 1):
            exchange(j, i).wait_recv()
        block = x[j].reshape(M, CW)
        gram[...] += dot(block, block, ((1,), (1,)))

    zs, peers = range(NZ - 1), range(len(PEERS))

    mine = pl.ds(pl.multiple_of(core * HALF, HALF), HALF)
    theirs = pl.ds(pl.multiple_of(other * HALF, HALF), HALF)
    swap_g = send(gram.at[theirs], core_g, send_c.at[0], recv_c.at[0], sibling)
    swap_g.start()

    part_y[...] = pack(dot(gram[...], initial[...], ((1,), (1,)))).reshape(
        2, CHIPS, 8, LANES
    )

    def scatter_y(n):
        to, at = peer(n)
        return to_peer(part_y.at[at, to], plane_y.at[n], 0, n)

    each(peers, scatter_y, started)

    swap_g.wait_recv()
    half_g[...] = gram[mine] + core_g[...]

    def scatter_g(k):
        rows = pl.ds(pl.multiple_of(chip_at(k) * SLAB, SLAB), SLAB)
        return to_chip(half_g.at[rows], plane_g.at[k], k)

    each(NEXT, scatter_g, started)

    each(peers, scatter_y, arrived)
    total = part_y[core, chip]
    for n in peers:
        total = total + plane_y[n]
    own_y[0] = total

    def z_send_y(i):
        return to_z(own_y.at[0], z_y.at[i], 0, i)

    each(zs, z_send_y, started)

    each(NEXT, scatter_g, arrived)
    total = half_g[pl.ds(pl.multiple_of(chip * SLAB, SLAB), SLAB)]
    for k in NEXT:
        total = total + plane_g[k]
    slab_g[...] = total

    def z_send_g(i):
        return to_z(slab_g, z_g.at[i], 1, i)

    each(zs, z_send_g, started)

    def z_sum(own, of):
        acc = None
        for z in range(NZ):
            value = own
            for i, offset in enumerate(OFFSETS):
                value = jnp.where(lax.rem(z + offset, NZ) == f, of[i], value)
            acc = value if acc is None else acc + value
        return acc

    each(zs, z_send_y, arrived)
    own_y[1] = z_sum(own_y[0], z_y)

    def gather_y(n):
        return to_peer(own_y.at[1], y_all.at[core, chip], 1, n)

    def gather_w(n):
        return to_peer(own_y.at[2], w_all.at[core, chip], 2, n)

    each(peers, gather_y, started)
    y_all[core, chip] = own_y[1]
    each(peers, gather_y, arrived)
    y1 = unpack(y_all[...].reshape(2 * CHIPS, 8, LANES))

    each(zs, z_send_g, arrived)
    own_g = z_sum(slab_g[...], z_g)
    own_y[2] = pack(dot(own_g, y1, ((1,), (0,))))[0]
    each(peers, gather_w, started)
    w_all[core, chip] = own_y[2]
    squares = dot(y1, y1, ((0,), (0,)))
    inverse1 = inverse_factor(jnp.concatenate([squares, squares], axis=1))
    each(peers, gather_w, arrived)

    w = unpack(w_all[...].reshape(2 * CHIPS, 8, LANES))
    y2 = dot(inverse1, w, ((1,), (1,)))
    squares = dot(y2, y2, ((1,), (1,)))
    inverse2 = inverse_factor(jnp.concatenate([squares, squares], axis=1))
    basis = dot(inverse2, y2, ((1,), (0,)))
    basis_out[...] = basis

    for j in range(0, CHUNKS, 2):
        pair = jnp.concatenate([x[j].reshape(M, CW), x[j + 1].reshape(M, CW)], axis=1)
        slab_out[:, j * CW : (j + 2) * CW] = dot(basis, pair, ((1,), (0,)))

    @pl.loop(0, CHUNKS)
    def _(j):
        for i in range(NZ - 1):
            exchange(j, i).wait_send()

    for make in (scatter_y, gather_y, gather_w):
        each(peers, make, left)
    for make in (z_send_y, z_send_g):
        each(zs, make, left)
    each(NEXT, scatter_g, left)
    swap_g.wait_send()


def shards(tensor, initial):
    vmem = pl.BlockSpec(memory_space=pltpu.VMEM)
    slab, basis = pl.pallas_call(
        kernel,
        name="subspace",
        out_shape=(
            jax.ShapeDtypeStruct((RANK, WIDTH), F32),
            jax.ShapeDtypeStruct((RANK, M), F32),
        ),
        in_specs=[pl.BlockSpec(memory_space=pl.ANY), vmem],
        out_specs=(vmem, vmem),
        scratch_shapes=[
            pltpu.VMEM((CHUNKS, NZ, ROWS, CW), F32),
            pltpu.VMEM((M, M), F32),
            pltpu.VMEM((HALF, M), F32),
            pltpu.VMEM((HALF, M), F32),
            pltpu.VMEM((CHIPS, SLAB, M), F32),
            pltpu.VMEM((SLAB, M), F32),
            pltpu.VMEM((NZ - 1, SLAB, M), F32),
            pltpu.VMEM((2, CHIPS, 8, LANES), F32),
            pltpu.VMEM((len(PEERS), 8, LANES), F32),
            pltpu.VMEM((NZ - 1, 8, LANES), F32),
            pltpu.VMEM((3, 8, LANES), F32),
            pltpu.VMEM((2, CHIPS, 8, LANES), F32),
            pltpu.VMEM((2, CHIPS, 8, LANES), F32),
            pltpu.SemaphoreType.DMA((CHUNKS,)),
            pltpu.SemaphoreType.DMA((CHUNKS, NZ - 1)),
            pltpu.SemaphoreType.DMA((CHUNKS, NZ - 1)),
            pltpu.SemaphoreType.DMA((CHIPS,)),
            pltpu.SemaphoreType.DMA((CHIPS,)),
            pltpu.SemaphoreType.DMA((3, len(PEERS))),
            pltpu.SemaphoreType.DMA((3, len(PEERS))),
            pltpu.SemaphoreType.DMA((2, NZ - 1)),
            pltpu.SemaphoreType.DMA((2, NZ - 1)),
            pltpu.SemaphoreType.DMA((1,)),
            pltpu.SemaphoreType.DMA((1,)),
        ],
        compiler_params=pltpu.CompilerParams(
            collective_id=0, has_side_effects=True, vmem_limit_bytes=51 * 1024 * 1024
        ),
    )(tensor, initial.T)
    return slab.reshape(RANK, 1, 1, WIDTH), basis.T


def solution(mesh):
    return jax.shard_map(
        shards,
        mesh=mesh,
        in_specs=(P("fibre", "cols", None, None), P()),
        out_specs=(P(None, "cols", "fibre", None), P()),
        check_vma=False,
    )
```

```python
import jax
import jax.numpy as jnp
from jax import lax
from jax.experimental import pallas as pl
from jax.experimental.pallas import tpu as pltpu
from jax.sharding import PartitionSpec as P

MESH = pl.DeviceIdType.MESH
HIGHEST = lax.Precision.HIGHEST
F32 = jnp.float32

M = 512
RANK = 64
WIDTH = 2048
NZ = 8
ROWS = M // NZ
CHIPS = 16
CHUNKS = 16
CW = WIDTH // CHUNKS
HALF = M // 2
SLAB = HALF // CHIPS
SIDES = 2
LANES = 128
OFFSETS = (4, 3, 5, 2, 6, 1, 7)


def hops(k):
    return min(k // 4, 4 - k // 4) + min(k % 4, 4 - k % 4)


NEXT = tuple(sorted(range(1, CHIPS), key=hops, reverse=True))
PEERS = tuple((k, o) for k in NEXT for o in (0, 1)) + ((0, 1),)


def dot(a, b, contract):
    return lax.dot_general(
        a, b, (contract, ((), ())), precision=HIGHEST, preferred_element_type=F32
    )


def augmented(squares):
    rows = lax.broadcasted_iota(jnp.int32, (RANK, LANES), 0)
    lanes = lax.broadcasted_iota(jnp.int32, (RANK, LANES), 1)
    return jnp.where(lanes < RANK, squares, (lanes - RANK == rows).astype(F32))


def inverse_factor(squares):
    rows = lax.broadcasted_iota(jnp.int32, (RANK, LANES), 0)
    top = lax.broadcasted_iota(jnp.int32, (8, LANES), 0)

    def panel(step, a):
        live = rows < RANK - 8 * step
        columns = [
            jnp.where(live, jnp.broadcast_to(a[:, t : t + 1], (RANK, LANES)), 0.0)
            for t in range(8)
        ]
        for t in range(8):
            pivot = columns[t][t : t + 1]
            inverse = 1.0 / pivot
            column = jnp.where(rows > t, columns[t], 0.0)
            row = a[t : t + 1]
            for q in range(t + 1, 8):
                columns[q] = columns[q] - column * (columns[q][t : t + 1] * inverse)
            a = a - column * (row * inverse)
            head = jnp.where(top == t, row * lax.rsqrt(pivot), a[:8])
            a = jnp.concatenate([head, a[8:]], axis=0)
        a = jnp.concatenate([a[8:], a[:8]], axis=0)
        return pltpu.roll(a, LANES - 8, 1)

    return lax.fori_loop(0, RANK // 8, panel, augmented(squares))[:, :RANK]


def pack(y):
    y = y.reshape(y.shape[0] // 16, 2, 8, RANK)
    return jnp.concatenate([y[:, 0], y[:, 1]], axis=2)


def unpack(y):
    n = y.shape[0]
    y = jnp.stack([y[:, :, :RANK], y[:, :, RANK:]], axis=1)
    return y.reshape(16 * n, RANK)


def kernel(
    tensor,
    initial,
    slab_out,
    basis_out,
    x,
    gram,
    core_g,
    half_g,
    plane_g,
    slab_g,
    z_g,
    part_y,
    plane_y,
    z_y,
    own_y,
    y_all,
    w_all,
    load_sem,
    send_x,
    recv_x,
    send_p,
    recv_p,
    send_d,
    recv_d,
    send_z,
    recv_z,
    send_c,
    recv_c,
):
    f, c = lax.axis_index("fibre"), lax.axis_index("cols")
    chip, core = c // 2, lax.rem(c, 2)
    chip_y, chip_x = chip // 4, lax.rem(chip, 4)
    other = 1 - core
    sibling = (f, chip * 2 + other)

    def z_at(offset):
        return lax.rem(f + offset, NZ)

    def chip_at(k):
        return lax.rem(chip_y + k // 4, 4) * 4 + lax.rem(chip_x + k % 4, 4)

    def send(src, dst, ssem, rsem, device):
        return pltpu.make_async_remote_copy(
            src_ref=src,
            dst_ref=dst,
            send_sem=ssem,
            recv_sem=rsem,
            device_id=device,
            device_id_type=MESH,
        )

    def piece(j, z):
        return tensor.at[:, 0, z, pl.ds(pl.multiple_of(j * CW, CW), CW)]

    def load_own(j):
        return pltpu.make_async_copy(piece(j, f), x.at[j, f], load_sem.at[j])

    def exchange(j, i):
        to = z_at(OFFSETS[i])
        return send(
            piece(j, to), x.at[j, f], send_x.at[j, i], recv_x.at[j, i], (to, c)
        )

    def peer(n):
        k, o = PEERS[n]
        return chip_at(k), other if o else core

    def to_peer(src, dst, which, n):
        to, at = peer(n)
        return send(
            src, dst, send_d.at[which, n], recv_d.at[which, n], (f, to * 2 + at)
        )

    def to_z(src, dst, which, i):
        return send(
            src, dst, send_z.at[which, i], recv_z.at[which, i], (z_at(OFFSETS[i]), c)
        )

    def each(order, make, act):
        for k in order:
            act(make(k))

    def started(copy):
        copy.start()

    def arrived(copy):
        copy.wait_recv()

    def left(copy):
        copy.wait_send()

    barrier = pltpu.get_barrier_semaphore()
    for offset in OFFSETS:
        pl.semaphore_signal(
            barrier, inc=1, device_id=(z_at(offset), c), device_id_type=MESH
        )
    for n in range(len(PEERS)):
        to, at = peer(n)
        pl.semaphore_signal(
            barrier, inc=1, device_id=(f, to * 2 + at), device_id_type=MESH
        )

    @pl.loop(0, CHUNKS)
    def _(j):
        load_own(j).start()

    gram[...] = jnp.zeros_like(gram)
    pl.semaphore_wait(barrier, NZ - 1 + len(PEERS))

    @pl.loop(0, CHUNKS)
    def _(j):
        for i in range(NZ - 1):
            exchange(j, i).start()

    @pl.loop(0, CHUNKS)
    def _(j):
        load_own(j).wait()
        for i in range(NZ - 1):
            exchange(j, i).wait_recv()
        block = x[j].reshape(M, CW)
        gram[...] += dot(block, block, ((1,), (1,)))

    zs, peers = range(NZ - 1), range(len(PEERS))

    mine = pl.ds(pl.multiple_of(core * HALF, HALF), HALF)
    theirs = pl.ds(pl.multiple_of(other * HALF, HALF), HALF)
    sides = tuple(pl.ds(h * M // SIDES, M // SIDES) for h in range(SIDES))

    def swap_g(h):
        return send(
            gram.at[theirs, sides[h]],
            core_g.at[:, sides[h]],
            send_c.at[h],
            recv_c.at[h],
            sibling,
        )

    each(range(SIDES), swap_g, started)

    part_y[...] = pack(dot(gram[...], initial[...], ((1,), (1,)))).reshape(
        2, CHIPS, 8, LANES
    )

    def scatter_y(n):
        to, at = peer(n)
        return to_peer(part_y.at[at, to], plane_y.at[n], 0, n)

    each(peers, scatter_y, started)

    def scatter_g(h, k):
        rows = pl.ds(pl.multiple_of(chip_at(k) * SLAB, SLAB), SLAB)
        return send(
            half_g.at[rows, sides[h]],
            plane_g.at[k, :, sides[h]],
            send_p.at[h, k],
            recv_p.at[h, k],
            (f, chip_at(k) * 2 + core),
        )

    for h in range(SIDES):
        swap_g(h).wait_recv()
        half_g[:, sides[h]] = gram[mine, sides[h]] + core_g[:, sides[h]]
        for k in NEXT:
            scatter_g(h, k).start()

    each(peers, scatter_y, arrived)
    total = part_y[core, chip]
    for n in peers:
        total = total + plane_y[n]
    own_y[0] = total

    def z_send_y(i):
        return to_z(own_y.at[0], z_y.at[i], 0, i)

    each(zs, z_send_y, started)

    def z_send_g(h, i):
        return to_z(
            slab_g.at[:, sides[h]], z_g.at[i, :, sides[h]], 1 + h, i
        )

    def on_to_z(h):
        own = pl.ds(pl.multiple_of(chip * SLAB, SLAB), SLAB)
        total = half_g[own, sides[h]]
        for k in NEXT:
            scatter_g(h, k).wait_recv()
        for k in NEXT:
            total = total + plane_g[k, :, sides[h]]
        slab_g[:, sides[h]] = total
        for i in zs:
            z_send_g(h, i).start()

    on_to_z(0)
    on_to_z(1)

    def z_sum(own, of):
        acc = None
        for z in range(NZ):
            value = own
            for i, offset in enumerate(OFFSETS):
                value = jnp.where(lax.rem(z + offset, NZ) == f, of[i], value)
            acc = value if acc is None else acc + value
        return acc

    each(zs, z_send_y, arrived)
    own_y[1] = z_sum(own_y[0], z_y)

    def gather_y(n):
        return to_peer(own_y.at[1], y_all.at[core, chip], 1, n)

    def gather_w(n):
        return to_peer(own_y.at[2], w_all.at[core, chip], 2, n)

    each(peers, gather_y, started)
    y_all[core, chip] = own_y[1]
    each(peers, gather_y, arrived)
    y1 = unpack(y_all[...].reshape(2 * CHIPS, 8, LANES))

    for h in range(SIDES):
        for i in zs:
            z_send_g(h, i).wait_recv()
    own_g = z_sum(slab_g[...], z_g)
    own_y[2] = pack(dot(own_g, y1, ((1,), (0,))))[0]
    each(peers, gather_w, started)
    w_all[core, chip] = own_y[2]
    squares = dot(y1, y1, ((0,), (0,)))
    inverse1 = inverse_factor(jnp.concatenate([squares, squares], axis=1))
    each(peers, gather_w, arrived)

    w = unpack(w_all[...].reshape(2 * CHIPS, 8, LANES))
    y2 = dot(inverse1, w, ((1,), (1,)))
    squares = dot(y2, y2, ((1,), (1,)))
    inverse2 = inverse_factor(jnp.concatenate([squares, squares], axis=1))
    basis = dot(inverse2, y2, ((1,), (0,)))
    basis_out[...] = basis

    for j in range(0, CHUNKS, 2):
        pair = jnp.concatenate([x[j].reshape(M, CW), x[j + 1].reshape(M, CW)], axis=1)
        slab_out[:, j * CW : (j + 2) * CW] = dot(basis, pair, ((1,), (0,)))

    @pl.loop(0, CHUNKS)
    def _(j):
        for i in range(NZ - 1):
            exchange(j, i).wait_send()

    for make in (scatter_y, gather_y, gather_w):
        each(peers, make, left)
    each(zs, z_send_y, left)
    for h in range(SIDES):
        swap_g(h).wait_send()
        for k in NEXT:
            scatter_g(h, k).wait_send()
        for i in zs:
            z_send_g(h, i).wait_send()


def shards(tensor, initial):
    vmem = pl.BlockSpec(memory_space=pltpu.VMEM)
    slab, basis = pl.pallas_call(
        kernel,
        name="subspace",
        out_shape=(
            jax.ShapeDtypeStruct((RANK, WIDTH), F32),
            jax.ShapeDtypeStruct((RANK, M), F32),
        ),
        in_specs=[pl.BlockSpec(memory_space=pl.ANY), vmem],
        out_specs=(vmem, vmem),
        scratch_shapes=[
            pltpu.VMEM((CHUNKS, NZ, ROWS, CW), F32),
            pltpu.VMEM((M, M), F32),
            pltpu.VMEM((HALF, M), F32),
            pltpu.VMEM((HALF, M), F32),
            pltpu.VMEM((CHIPS, SLAB, M), F32),
            pltpu.VMEM((SLAB, M), F32),
            pltpu.VMEM((NZ - 1, SLAB, M), F32),
            pltpu.VMEM((2, CHIPS, 8, LANES), F32),
            pltpu.VMEM((len(PEERS), 8, LANES), F32),
            pltpu.VMEM((NZ - 1, 8, LANES), F32),
            pltpu.VMEM((3, 8, LANES), F32),
            pltpu.VMEM((2, CHIPS, 8, LANES), F32),
            pltpu.VMEM((2, CHIPS, 8, LANES), F32),
            pltpu.SemaphoreType.DMA((CHUNKS,)),
            pltpu.SemaphoreType.DMA((CHUNKS, NZ - 1)),
            pltpu.SemaphoreType.DMA((CHUNKS, NZ - 1)),
            pltpu.SemaphoreType.DMA((SIDES, CHIPS)),
            pltpu.SemaphoreType.DMA((SIDES, CHIPS)),
            pltpu.SemaphoreType.DMA((3, len(PEERS))),
            pltpu.SemaphoreType.DMA((3, len(PEERS))),
            pltpu.SemaphoreType.DMA((1 + SIDES, NZ - 1)),
            pltpu.SemaphoreType.DMA((1 + SIDES, NZ - 1)),
            pltpu.SemaphoreType.DMA((SIDES,)),
            pltpu.SemaphoreType.DMA((SIDES,)),
        ],
        compiler_params=pltpu.CompilerParams(
            collective_id=0, has_side_effects=True, vmem_limit_bytes=51 * 1024 * 1024
        ),
    )(tensor, initial.T)
    return slab.reshape(RANK, 1, 1, WIDTH), basis.T


def solution(mesh):
    return jax.shard_map(
        shards,
        mesh=mesh,
        in_specs=(P("fibre", "cols", None, None), P()),
        out_specs=(P(None, "cols", "fibre", None), P()),
        check_vma=False,
    )
```

```python
import jax
import jax.numpy as jnp
from jax import lax
from jax.experimental import pallas as pl
from jax.experimental.pallas import tpu as pltpu
from jax.sharding import PartitionSpec as P

MESH = pl.DeviceIdType.MESH
HIGHEST = lax.Precision.HIGHEST
F32 = jnp.float32

M = 512
RANK = 64
WIDTH = 2048
NZ = 8
ROWS = M // NZ
CHIPS = 16
CHUNKS = 16
CW = WIDTH // CHUNKS
HALF = M // 2
SLAB = HALF // CHIPS
SIDES = 2
LANES = 128
OFFSETS = (4, 3, 5, 2, 6, 1, 7)


def hops(k):
    return min(k // 4, 4 - k // 4) + min(k % 4, 4 - k % 4)


NEXT = tuple(sorted(range(1, CHIPS), key=hops, reverse=True))
PEERS = tuple((k, o) for k in NEXT for o in (0, 1)) + ((0, 1),)


def dot(a, b, contract):
    return lax.dot_general(
        a, b, (contract, ((), ())), precision=HIGHEST, preferred_element_type=F32
    )


def augmented(squares):
    rows = lax.broadcasted_iota(jnp.int32, (RANK, LANES), 0)
    lanes = lax.broadcasted_iota(jnp.int32, (RANK, LANES), 1)
    return jnp.where(lanes < RANK, squares, (lanes - RANK == rows).astype(F32))


def inverse_factor(squares):
    rows = lax.broadcasted_iota(jnp.int32, (RANK, LANES), 0)
    top = lax.broadcasted_iota(jnp.int32, (8, LANES), 0)

    def panel(step, a):
        live = rows < RANK - 8 * step
        columns = [
            jnp.where(live, jnp.broadcast_to(a[:, t : t + 1], (RANK, LANES)), 0.0)
            for t in range(8)
        ]
        for t in range(8):
            pivot = columns[t][t : t + 1]
            inverse = 1.0 / pivot
            column = jnp.where(rows > t, columns[t], 0.0)
            row = a[t : t + 1]
            for q in range(t + 1, 8):
                columns[q] = columns[q] - column * (columns[q][t : t + 1] * inverse)
            a = a - column * (row * inverse)
            head = jnp.where(top == t, row * lax.rsqrt(pivot), a[:8])
            a = jnp.concatenate([head, a[8:]], axis=0)
        a = jnp.concatenate([a[8:], a[:8]], axis=0)
        return pltpu.roll(a, LANES - 8, 1)

    return lax.fori_loop(0, RANK // 8, panel, augmented(squares))[:, :RANK]


def pack(y):
    y = y.reshape(y.shape[0] // 16, 2, 8, RANK)
    return jnp.concatenate([y[:, 0], y[:, 1]], axis=2)


def unpack(y):
    n = y.shape[0]
    y = jnp.stack([y[:, :, :RANK], y[:, :, RANK:]], axis=1)
    return y.reshape(16 * n, RANK)


def kernel(
    tensor,
    initial,
    slab_out,
    basis_out,
    x,
    gram,
    core_g,
    half_g,
    plane_g,
    slab_g,
    z_g,
    part_y,
    plane_y,
    z_y,
    own_y,
    y_all,
    w_all,
    load_sem,
    send_x,
    recv_x,
    send_p,
    recv_p,
    send_d,
    recv_d,
    send_z,
    recv_z,
    send_c,
    recv_c,
):
    f, c = lax.axis_index("fibre"), lax.axis_index("cols")
    chip, core = c // 2, lax.rem(c, 2)
    chip_y, chip_x = chip // 4, lax.rem(chip, 4)
    other = 1 - core
    sibling = (f, chip * 2 + other)

    def z_at(offset):
        return lax.rem(f + offset, NZ)

    def chip_at(k):
        return lax.rem(chip_y + k // 4, 4) * 4 + lax.rem(chip_x + k % 4, 4)

    def send(src, dst, ssem, rsem, device):
        return pltpu.make_async_remote_copy(
            src_ref=src,
            dst_ref=dst,
            send_sem=ssem,
            recv_sem=rsem,
            device_id=device,
            device_id_type=MESH,
        )

    def piece(j, z):
        return tensor.at[:, 0, z, pl.ds(pl.multiple_of(j * CW, CW), CW)]

    def load_own(j):
        return pltpu.make_async_copy(piece(j, f), x.at[j, f], load_sem.at[j])

    def exchange(j, i):
        to = z_at(OFFSETS[i])
        return send(
            piece(j, to), x.at[j, f], send_x.at[j, i], recv_x.at[j, i], (to, c)
        )

    def peer(n):
        k, o = PEERS[n]
        return chip_at(k), other if o else core

    def to_peer(src, dst, which, n):
        to, at = peer(n)
        return send(
            src, dst, send_d.at[which, n], recv_d.at[which, n], (f, to * 2 + at)
        )

    def to_z(src, dst, which, i):
        return send(
            src, dst, send_z.at[which, i], recv_z.at[which, i], (z_at(OFFSETS[i]), c)
        )

    def each(order, make, act):
        for k in order:
            act(make(k))

    def started(copy):
        copy.start()

    def arrived(copy):
        copy.wait_recv()

    def left(copy):
        copy.wait_send()

    barrier = pltpu.get_barrier_semaphore()
    for offset in OFFSETS:
        pl.semaphore_signal(
            barrier, inc=1, device_id=(z_at(offset), c), device_id_type=MESH
        )
    for n in range(len(PEERS)):
        to, at = peer(n)
        pl.semaphore_signal(
            barrier, inc=1, device_id=(f, to * 2 + at), device_id_type=MESH
        )

    @pl.loop(0, CHUNKS)
    def _(j):
        load_own(j).start()

    gram[...] = jnp.zeros_like(gram)
    pl.semaphore_wait(barrier, NZ - 1 + len(PEERS))

    @pl.loop(0, CHUNKS)
    def _(j):
        for i in range(NZ - 1):
            exchange(j, i).start()

    @pl.loop(0, CHUNKS)
    def _(j):
        load_own(j).wait()
        for i in range(NZ - 1):
            exchange(j, i).wait_recv()
        block = x[j].reshape(M, CW)
        gram[...] += dot(block, block, ((1,), (1,)))

    zs, peers = range(NZ - 1), range(len(PEERS))

    mine = pl.ds(pl.multiple_of(core * HALF, HALF), HALF)
    theirs = pl.ds(pl.multiple_of(other * HALF, HALF), HALF)
    sides = tuple(pl.ds(h * M // SIDES, M // SIDES) for h in range(SIDES))

    def swap_g(h):
        return send(
            gram.at[theirs, sides[h]],
            core_g.at[:, sides[h]],
            send_c.at[h],
            recv_c.at[h],
            sibling,
        )

    each(range(SIDES), swap_g, started)

    part_y[...] = pack(dot(gram[...], initial[...], ((1,), (1,)))).reshape(
        2, CHIPS, 8, LANES
    )

    def scatter_y(n):
        to, at = peer(n)
        return to_peer(part_y.at[at, to], plane_y.at[n], 0, n)

    each(peers, scatter_y, started)

    def scatter_g(h, k):
        rows = pl.ds(pl.multiple_of(chip_at(k) * SLAB, SLAB), SLAB)
        return send(
            half_g.at[rows, sides[h]],
            plane_g.at[k, :, sides[h]],
            send_p.at[h, k],
            recv_p.at[h, k],
            (f, chip_at(k) * 2 + core),
        )

    for h in range(SIDES):
        swap_g(h).wait_recv()
        half_g[:, sides[h]] = gram[mine, sides[h]] + core_g[:, sides[h]]
        for k in NEXT:
            scatter_g(h, k).start()

    each(peers, scatter_y, arrived)
    total = part_y[core, chip]
    for n in peers:
        total = total + plane_y[n]
    own_y[0] = total

    def z_send_y(i):
        return to_z(own_y.at[0], z_y.at[i], 0, i)

    each(zs, z_send_y, started)

    def z_send_g(h, i):
        return to_z(
            slab_g.at[:, sides[h]], z_g.at[i, :, sides[h]], 1 + h, i
        )

    def on_to_z(h):
        own = pl.ds(pl.multiple_of(chip * SLAB, SLAB), SLAB)
        total = half_g[own, sides[h]]
        for k in NEXT:
            scatter_g(h, k).wait_recv()
        for k in NEXT:
            total = total + plane_g[k, :, sides[h]]
        slab_g[:, sides[h]] = total
        for i in zs:
            z_send_g(h, i).start()

    @pl.loop(0, CHUNKS)
    def _(j):
        for i in range(NZ - 1):
            exchange(j, i).wait_send()

    on_to_z(0)
    on_to_z(1)

    def z_sum(own, of):
        acc = None
        for z in range(NZ):
            value = own
            for i, offset in enumerate(OFFSETS):
                value = jnp.where(lax.rem(z + offset, NZ) == f, of[i], value)
            acc = value if acc is None else acc + value
        return acc

    each(zs, z_send_y, arrived)
    own_y[1] = z_sum(own_y[0], z_y)

    def gather_y(n):
        return to_peer(own_y.at[1], y_all.at[core, chip], 1, n)

    def gather_w(n):
        return to_peer(own_y.at[2], w_all.at[core, chip], 2, n)

    each(peers, gather_y, started)
    y_all[core, chip] = own_y[1]
    each(peers, scatter_y, left)
    each(zs, z_send_y, left)
    for h in range(SIDES):
        swap_g(h).wait_send()
        for k in NEXT:
            scatter_g(h, k).wait_send()

    each(peers, gather_y, arrived)
    y1 = unpack(y_all[...].reshape(2 * CHIPS, 8, LANES))

    for h in range(SIDES):
        for i in zs:
            z_send_g(h, i).wait_recv()
    own_g = z_sum(slab_g[...], z_g)
    own_y[2] = pack(dot(own_g, y1, ((1,), (0,))))[0]
    each(peers, gather_w, started)
    w_all[core, chip] = own_y[2]
    squares = dot(y1, y1, ((0,), (0,)))
    inverse1 = inverse_factor(jnp.concatenate([squares, squares], axis=1))
    each(peers, gather_y, left)
    for h in range(SIDES):
        for i in zs:
            z_send_g(h, i).wait_send()

    each(peers, gather_w, arrived)

    w = unpack(w_all[...].reshape(2 * CHIPS, 8, LANES))
    y2 = dot(inverse1, w, ((1,), (1,)))
    squares = dot(y2, y2, ((1,), (1,)))
    inverse2 = inverse_factor(jnp.concatenate([squares, squares], axis=1))
    basis = dot(inverse2, y2, ((1,), (0,)))
    basis_out[...] = basis

    for j in range(0, CHUNKS, 2):
        pair = jnp.concatenate([x[j].reshape(M, CW), x[j + 1].reshape(M, CW)], axis=1)
        columns = dot(basis, pair, ((1,), (0,)))
        slab_out[:, j, :] = columns[:, :CW]
        slab_out[:, j + 1, :] = columns[:, CW:]

    each(peers, gather_w, left)


def shards(tensor, initial):
    vmem = pl.BlockSpec(memory_space=pltpu.VMEM)
    slab, basis = pl.pallas_call(
        kernel,
        name="subspace",
        out_shape=(
            jax.ShapeDtypeStruct((RANK, CHUNKS, CW), F32),
            jax.ShapeDtypeStruct((RANK, M), F32),
        ),
        in_specs=[pl.BlockSpec(memory_space=pl.ANY), vmem],
        out_specs=(vmem, vmem),
        scratch_shapes=[
            pltpu.VMEM((CHUNKS, NZ, ROWS, CW), F32),
            pltpu.VMEM((M, M), F32),
            pltpu.VMEM((HALF, M), F32),
            pltpu.VMEM((HALF, M), F32),
            pltpu.VMEM((CHIPS, SLAB, M), F32),
            pltpu.VMEM((SLAB, M), F32),
            pltpu.VMEM((NZ - 1, SLAB, M), F32),
            pltpu.VMEM((2, CHIPS, 8, LANES), F32),
            pltpu.VMEM((len(PEERS), 8, LANES), F32),
            pltpu.VMEM((NZ - 1, 8, LANES), F32),
            pltpu.VMEM((3, 8, LANES), F32),
            pltpu.VMEM((2, CHIPS, 8, LANES), F32),
            pltpu.VMEM((2, CHIPS, 8, LANES), F32),
            pltpu.SemaphoreType.DMA((CHUNKS,)),
            pltpu.SemaphoreType.DMA((CHUNKS, NZ - 1)),
            pltpu.SemaphoreType.DMA((CHUNKS, NZ - 1)),
            pltpu.SemaphoreType.DMA((SIDES, CHIPS)),
            pltpu.SemaphoreType.DMA((SIDES, CHIPS)),
            pltpu.SemaphoreType.DMA((3, len(PEERS))),
            pltpu.SemaphoreType.DMA((3, len(PEERS))),
            pltpu.SemaphoreType.DMA((1 + SIDES, NZ - 1)),
            pltpu.SemaphoreType.DMA((1 + SIDES, NZ - 1)),
            pltpu.SemaphoreType.DMA((SIDES,)),
            pltpu.SemaphoreType.DMA((SIDES,)),
        ],
        compiler_params=pltpu.CompilerParams(
            collective_id=0, has_side_effects=True, vmem_limit_bytes=51 * 1024 * 1024
        ),
    )(tensor, initial.T)
    return slab.reshape(RANK, 1, 1, WIDTH), basis.T


def solution(mesh):
    return jax.shard_map(
        shards,
        mesh=mesh,
        in_specs=(P("fibre", "cols", None, None), P()),
        out_specs=(P(None, "cols", "fibre", None), P()),
        check_vma=False,
    )
```

```python
import jax
import jax.numpy as jnp
from jax import lax
from jax.experimental import pallas as pl
from jax.experimental.pallas import tpu as pltpu
from jax.sharding import PartitionSpec as P

MESH = pl.DeviceIdType.MESH
HIGHEST = lax.Precision.HIGHEST
F32 = jnp.float32

M = 512
RANK = 64
WIDTH = 2048
NZ = 8
ROWS = M // NZ
CHIPS = 16
CHUNKS = 16
CW = WIDTH // CHUNKS
HALF = M // 2
SLAB = HALF // CHIPS
SIDES = 2
LANES = 128
OFFSETS = (4, 3, 5, 2, 6, 1, 7)


def hops(k):
    return min(k // 4, 4 - k // 4) + min(k % 4, 4 - k % 4)


NEXT = tuple(sorted(range(1, CHIPS), key=hops, reverse=True))
PEERS = tuple((k, o) for k in NEXT for o in (0, 1)) + ((0, 1),)


def dot(a, b, contract):
    return lax.dot_general(
        a, b, (contract, ((), ())), precision=HIGHEST, preferred_element_type=F32
    )


def halves(value):
    high = value.astype(jnp.bfloat16)
    return high, (value - high.astype(F32)).astype(jnp.bfloat16)


def augmented(squares):
    rows = lax.broadcasted_iota(jnp.int32, (RANK, LANES), 0)
    lanes = lax.broadcasted_iota(jnp.int32, (RANK, LANES), 1)
    return jnp.where(lanes < RANK, squares, (lanes - RANK == rows).astype(F32))


def inverse_factor(squares):
    rows = lax.broadcasted_iota(jnp.int32, (RANK, LANES), 0)
    top = lax.broadcasted_iota(jnp.int32, (8, LANES), 0)

    def panel(step, a):
        live = rows < RANK - 8 * step
        columns = [
            jnp.where(live, jnp.broadcast_to(a[:, t : t + 1], (RANK, LANES)), 0.0)
            for t in range(8)
        ]
        for t in range(8):
            pivot = columns[t][t : t + 1]
            inverse = 1.0 / pivot
            column = jnp.where(rows > t, columns[t], 0.0)
            row = a[t : t + 1]
            for q in range(t + 1, 8):
                columns[q] = columns[q] - column * (columns[q][t : t + 1] * inverse)
            a = a - column * (row * inverse)
            head = jnp.where(top == t, row * lax.rsqrt(pivot), a[:8])
            a = jnp.concatenate([head, a[8:]], axis=0)
        a = jnp.concatenate([a[8:], a[:8]], axis=0)
        return pltpu.roll(a, LANES - 8, 1)

    return lax.fori_loop(0, RANK // 8, panel, augmented(squares))[:, :RANK]


def pack(y):
    y = y.reshape(y.shape[0] // 16, 2, 8, RANK)
    return jnp.concatenate([y[:, 0], y[:, 1]], axis=2)


def unpack(y):
    n = y.shape[0]
    y = jnp.stack([y[:, :, :RANK], y[:, :, RANK:]], axis=1)
    return y.reshape(16 * n, RANK)


def kernel(
    tensor,
    initial,
    slab_out,
    basis_out,
    x,
    gram,
    core_g,
    half_g,
    plane_g,
    slab_g,
    z_g,
    part_y,
    plane_y,
    z_y,
    own_y,
    y_all,
    w_all,
    load_sem,
    send_x,
    recv_x,
    send_p,
    recv_p,
    send_d,
    recv_d,
    send_z,
    recv_z,
    send_c,
    recv_c,
):
    f, c = lax.axis_index("fibre"), lax.axis_index("cols")
    chip, core = c // 2, lax.rem(c, 2)
    chip_y, chip_x = chip // 4, lax.rem(chip, 4)
    other = 1 - core
    sibling = (f, chip * 2 + other)

    def z_at(offset):
        return lax.rem(f + offset, NZ)

    def chip_at(k):
        return lax.rem(chip_y + k // 4, 4) * 4 + lax.rem(chip_x + k % 4, 4)

    def send(src, dst, ssem, rsem, device):
        return pltpu.make_async_remote_copy(
            src_ref=src,
            dst_ref=dst,
            send_sem=ssem,
            recv_sem=rsem,
            device_id=device,
            device_id_type=MESH,
        )

    def piece(j, z):
        return tensor.at[:, 0, z, pl.ds(pl.multiple_of(j * CW, CW), CW)]

    def load_own(j):
        return pltpu.make_async_copy(piece(j, f), x.at[j, f], load_sem.at[j])

    def exchange(j, i):
        to = z_at(OFFSETS[i])
        return send(
            piece(j, to), x.at[j, f], send_x.at[j, i], recv_x.at[j, i], (to, c)
        )

    def peer(n):
        k, o = PEERS[n]
        return chip_at(k), other if o else core

    def to_peer(src, dst, which, n):
        to, at = peer(n)
        return send(
            src, dst, send_d.at[which, n], recv_d.at[which, n], (f, to * 2 + at)
        )

    def to_z(src, dst, which, i):
        return send(
            src, dst, send_z.at[which, i], recv_z.at[which, i], (z_at(OFFSETS[i]), c)
        )

    def each(order, make, act):
        for k in order:
            act(make(k))

    def started(copy):
        copy.start()

    def arrived(copy):
        copy.wait_recv()

    def left(copy):
        copy.wait_send()

    barrier = pltpu.get_barrier_semaphore()
    for offset in OFFSETS:
        pl.semaphore_signal(
            barrier, inc=1, device_id=(z_at(offset), c), device_id_type=MESH
        )
    for n in range(len(PEERS)):
        to, at = peer(n)
        pl.semaphore_signal(
            barrier, inc=1, device_id=(f, to * 2 + at), device_id_type=MESH
        )

    @pl.loop(0, CHUNKS)
    def _(j):
        load_own(j).start()

    gram[...] = jnp.zeros_like(gram)
    pl.semaphore_wait(barrier, NZ - 1 + len(PEERS))

    @pl.loop(0, CHUNKS)
    def _(j):
        for i in range(NZ - 1):
            exchange(j, i).start()

    @pl.loop(0, CHUNKS)
    def _(j):
        load_own(j).wait()
        for i in range(NZ - 1):
            exchange(j, i).wait_recv()
        block = x[j].reshape(M, CW)
        gram[...] += dot(block, block, ((1,), (1,)))

    zs, peers = range(NZ - 1), range(len(PEERS))

    mine = pl.ds(pl.multiple_of(core * HALF, HALF), HALF)
    theirs = pl.ds(pl.multiple_of(other * HALF, HALF), HALF)
    sides = tuple(pl.ds(h * M // SIDES, M // SIDES) for h in range(SIDES))

    def swap_g(h):
        return send(
            gram.at[theirs, sides[h]],
            core_g.at[:, sides[h]],
            send_c.at[h],
            recv_c.at[h],
            sibling,
        )

    each(range(SIDES), swap_g, started)

    part_y[...] = pack(dot(gram[...], initial[...], ((1,), (1,)))).reshape(
        2, CHIPS, 8, LANES
    )

    def scatter_y(n):
        to, at = peer(n)
        return to_peer(part_y.at[at, to], plane_y.at[n], 0, n)

    each(peers, scatter_y, started)

    def scatter_g(h, k):
        rows = pl.ds(pl.multiple_of(chip_at(k) * SLAB, SLAB), SLAB)
        return send(
            half_g.at[rows, sides[h]],
            plane_g.at[k, :, sides[h]],
            send_p.at[h, k],
            recv_p.at[h, k],
            (f, chip_at(k) * 2 + core),
        )

    for h in range(SIDES):
        swap_g(h).wait_recv()
        half_g[:, sides[h]] = gram[mine, sides[h]] + core_g[:, sides[h]]
        for k in NEXT:
            scatter_g(h, k).start()

    each(peers, scatter_y, arrived)
    total = part_y[core, chip]
    for n in peers:
        total = total + plane_y[n]
    own_y[0] = total

    def z_send_y(i):
        return to_z(own_y.at[0], z_y.at[i], 0, i)

    each(zs, z_send_y, started)

    def z_send_g(h, i):
        return to_z(
            slab_g.at[:, sides[h]], z_g.at[i, :, sides[h]], 1 + h, i
        )

    def on_to_z(h):
        own = pl.ds(pl.multiple_of(chip * SLAB, SLAB), SLAB)
        total = half_g[own, sides[h]]
        for k in NEXT:
            scatter_g(h, k).wait_recv()
        for k in NEXT:
            total = total + plane_g[k, :, sides[h]]
        slab_g[:, sides[h]] = total
        for i in zs:
            z_send_g(h, i).start()

    @pl.loop(0, CHUNKS)
    def _(j):
        for i in range(NZ - 1):
            exchange(j, i).wait_send()

    on_to_z(0)
    on_to_z(1)

    def z_sum(own, of):
        acc = None
        for z in range(NZ):
            value = own
            for i, offset in enumerate(OFFSETS):
                value = jnp.where(lax.rem(z + offset, NZ) == f, of[i], value)
            acc = value if acc is None else acc + value
        return acc

    each(zs, z_send_y, arrived)
    own_y[1] = z_sum(own_y[0], z_y)

    def gather_y(n):
        return to_peer(own_y.at[1], y_all.at[core, chip], 1, n)

    def gather_w(n):
        return to_peer(own_y.at[2], w_all.at[core, chip], 2, n)

    each(peers, gather_y, started)
    y_all[core, chip] = own_y[1]
    each(peers, scatter_y, left)
    each(zs, z_send_y, left)
    for h in range(SIDES):
        swap_g(h).wait_send()
        for k in NEXT:
            scatter_g(h, k).wait_send()

    each(peers, gather_y, arrived)
    y1 = unpack(y_all[...].reshape(2 * CHIPS, 8, LANES))

    for h in range(SIDES):
        for i in zs:
            z_send_g(h, i).wait_recv()
    own_g = z_sum(slab_g[...], z_g)
    own_y[2] = pack(dot(own_g, y1, ((1,), (0,))))[0]
    each(peers, gather_w, started)
    w_all[core, chip] = own_y[2]
    squares = dot(y1, y1, ((0,), (0,)))
    inverse1 = inverse_factor(jnp.concatenate([squares, squares], axis=1))
    each(peers, gather_y, left)
    for h in range(SIDES):
        for i in zs:
            z_send_g(h, i).wait_send()

    each(peers, gather_w, arrived)

    w = unpack(w_all[...].reshape(2 * CHIPS, 8, LANES))
    y2 = dot(inverse1, w, ((1,), (1,)))
    squares = dot(y2, y2, ((1,), (1,)))
    inverse2 = inverse_factor(jnp.concatenate([squares, squares], axis=1))
    basis = dot(inverse2, y2, ((1,), (0,)))
    basis_out[...] = basis

    high, low = halves(basis)
    left_side = jnp.concatenate([high, high, low], axis=1)
    for j in range(0, CHUNKS, 2):
        pair = jnp.concatenate([x[j].reshape(M, CW), x[j + 1].reshape(M, CW)], axis=1)
        high, low = halves(pair)
        columns = jnp.dot(
            left_side,
            jnp.concatenate([high, low, high], axis=0),
            preferred_element_type=F32,
        )
        slab_out[:, j, :] = columns[:, :CW]
        slab_out[:, j + 1, :] = columns[:, CW:]

    each(peers, gather_w, left)


def shards(tensor, initial):
    vmem = pl.BlockSpec(memory_space=pltpu.VMEM)
    slab, basis = pl.pallas_call(
        kernel,
        name="subspace",
        out_shape=(
            jax.ShapeDtypeStruct((RANK, CHUNKS, CW), F32),
            jax.ShapeDtypeStruct((RANK, M), F32),
        ),
        in_specs=[pl.BlockSpec(memory_space=pl.ANY), vmem],
        out_specs=(vmem, vmem),
        scratch_shapes=[
            pltpu.VMEM((CHUNKS, NZ, ROWS, CW), F32),
            pltpu.VMEM((M, M), F32),
            pltpu.VMEM((HALF, M), F32),
            pltpu.VMEM((HALF, M), F32),
            pltpu.VMEM((CHIPS, SLAB, M), F32),
            pltpu.VMEM((SLAB, M), F32),
            pltpu.VMEM((NZ - 1, SLAB, M), F32),
            pltpu.VMEM((2, CHIPS, 8, LANES), F32),
            pltpu.VMEM((len(PEERS), 8, LANES), F32),
            pltpu.VMEM((NZ - 1, 8, LANES), F32),
            pltpu.VMEM((3, 8, LANES), F32),
            pltpu.VMEM((2, CHIPS, 8, LANES), F32),
            pltpu.VMEM((2, CHIPS, 8, LANES), F32),
            pltpu.SemaphoreType.DMA((CHUNKS,)),
            pltpu.SemaphoreType.DMA((CHUNKS, NZ - 1)),
            pltpu.SemaphoreType.DMA((CHUNKS, NZ - 1)),
            pltpu.SemaphoreType.DMA((SIDES, CHIPS)),
            pltpu.SemaphoreType.DMA((SIDES, CHIPS)),
            pltpu.SemaphoreType.DMA((3, len(PEERS))),
            pltpu.SemaphoreType.DMA((3, len(PEERS))),
            pltpu.SemaphoreType.DMA((1 + SIDES, NZ - 1)),
            pltpu.SemaphoreType.DMA((1 + SIDES, NZ - 1)),
            pltpu.SemaphoreType.DMA((SIDES,)),
            pltpu.SemaphoreType.DMA((SIDES,)),
        ],
        compiler_params=pltpu.CompilerParams(
            collective_id=0, has_side_effects=True, vmem_limit_bytes=51 * 1024 * 1024
        ),
    )(tensor, initial.T)
    return slab.reshape(RANK, 1, 1, WIDTH), basis.T


def solution(mesh):
    return jax.shard_map(
        shards,
        mesh=mesh,
        in_specs=(P("fibre", "cols", None, None), P()),
        out_specs=(P(None, "cols", "fibre", None), P()),
        check_vma=False,
    )
```
